32 devices in a mesh: groups: 1, wide: 32 (over z, y, x, core), narrow: 1.
Axes of the slice: x: 2, y: 2, z: 4, core: 2. Of those that a mesh axis runs over, the one named last changes fastest.
Arguments:
- gamma_tensor: bfloat16 [256, 128, 1024], P(('groups', 'wide'), None, 'narrow'), may hold values from -6 to 6
- three_center: bfloat16 [256, 128, 1024], P(('groups', 'wide'), None, 'narrow'), may hold values from -6 to 6
- gamma_blocks: int32 [256, 2, 16], P(('groups', 'wide'), None, 'narrow'), may hold values 0 or 1
- center_blocks: int32 [256, 2, 16], P(('groups', 'wide'), None, 'narrow'), may hold values 0 or 1
Outputs:
- density_occ: float32 [128, 128], P(('groups', 'wide', 'narrow'))
- gamma_aux: float32 [256, 256], P(('groups', 'wide', 'narrow'))
The draws below stay inside these ranges and needn't reach their ends.
All inputs are finite; a program needn't handle non-finite values. No bound on the sum of `gamma_blocks` or of `center_blocks` on one device may be relied on, other than what follows from the above.
Results may differ from the reference program's by a relative error of at most 0.0003.
Values may be sent and summed in bfloat16 or wider, within the bound.
A program may use at most 64 MiB of HBM per device.

```python
import math
import jax
import jax.numpy as jnp
from jax import lax

BLK = 64
NVIR = 1024
NAUX = 256
NOCC = 128


def touch_ends(result, own_key, smallest, high):
    place = [jax.random.randint(jax.random.fold_in(own_key, axis), (), 0, length) for axis, length in enumerate(result.shape)]
    widest = result.shape.index(max(result.shape))
    beside = place[:widest] + [(place[widest] + 1) % result.shape[widest]] + place[widest + 1:]
    return result.at[tuple(place)].set(smallest).at[tuple(beside)].set(high)


def strengthened(array, key, source, target, parts, factor):
    owner, partner = [(jnp.arange(array.shape[axis_at]) // (array.shape[axis_at] // parts)).reshape([-1 if axis == axis_at else 1 for axis in range(array.ndim)]) for axis_at in (source, target)]
    chosen = jax.random.permutation(key, parts)[partner]
    strong = (owner == chosen) | (owner == (partner + parts // 2) % parts)
    return jnp.where(strong, factor * array, array)


def block_scale(rng, dims, pieces, least, largest):
    def one(dim, shards_of):
        draws = jax.random.uniform(jax.random.fold_in(jax.random.fold_in(rng, 6), dim), (shards_of,), jnp.float32, least / len(pieces), largest / len(pieces))
        return jnp.repeat(jnp.exp(draws), dims[dim] // shards_of).reshape((-1,) + (1,) * (len(dims) - dim - 1))

    gain = one(*pieces[0])
    for cut in pieces[1:]:
        gain = gain * one(*cut)
    return gain


def noise_with(own_key, extent, width, reach, cuts, heavy, kind=jnp.bfloat16):
    array = width * jax.random.normal(own_key, extent, jnp.float32)
    if cuts:
        array = array * block_scale(own_key, extent, cuts, -0.22, 0.18)
    return jnp.clip(strengthened(array, jax.random.fold_in(own_key, 3), *heavy), -reach, reach).astype(kind)


def setup_inputs(seed: int = 0, part: int = 0) -> dict:
    splits = jax.random.split(jax.random.key(seed), 5)
    part_splits = jax.random.split(jax.random.fold_in(splits[4], part), 5)
    return {
        "gamma_tensor": noise_with(part_splits[0], (NAUX, NOCC, NVIR), 1.0, 6.0, ((0, 32),), (0, 1, 32, 2.75)),
        "three_center": noise_with(part_splits[1], (NAUX, NOCC, NVIR), 1.0, 6.0, ((0, 32),), (1, 0, 32, 2.75)),
        "gamma_blocks": touch_ends((jax.random.randint(part_splits[2], (NAUX, NOCC // BLK, NVIR // BLK), 0, 4) < 3).astype(jnp.int32), jax.random.fold_in(part_splits[2], 1), 0, 1),
        "center_blocks": touch_ends((jax.random.randint(part_splits[3], (NAUX, NOCC // BLK, NVIR // BLK), 0, 4) < 3).astype(jnp.int32), jax.random.fold_in(part_splits[3], 1), 0, 1),
    }


def apply_blocks(tensor, block_mask):
    aux_rows, occ_cols, vir_cols = tensor.shape
    shaped = tensor.reshape(aux_rows, occ_cols // BLK, BLK, vir_cols // BLK, BLK)
    factor = block_mask.astype(tensor.dtype)[:, :, None, :, None]
    return (shaped * factor).reshape(aux_rows, occ_cols, vir_cols)

def reference(gamma_tensor, three_center, gamma_blocks, center_blocks):
    gamma_full = apply_blocks(gamma_tensor, gamma_blocks)
    center_full = apply_blocks(three_center, center_blocks)
    occ_scale = -1.0 / math.sqrt(NAUX * NVIR)
    aux_scale = 1.0 / math.sqrt(NOCC * NVIR)
    density_occ = lax.dot_general(gamma_full, center_full, (((0, 2), (0, 2)), ((), ())), preferred_element_type=jnp.float32) * occ_scale
    gamma_aux = lax.dot_general(gamma_full, center_full, (((1, 2), (1, 2)), ((), ())), preferred_element_type=jnp.float32) * aux_scale
    return (density_occ, gamma_aux)
```

```python
import math

import jax
import jax.numpy as jnp
from jax import lax
from jax.sharding import PartitionSpec as P

BLK = 64


def apply_blocks(tensor, block_mask):
    aux_rows, occ_cols, vir_cols = tensor.shape
    shaped = tensor.reshape(aux_rows, occ_cols // BLK, BLK, vir_cols // BLK, BLK)
    factor = block_mask.astype(tensor.dtype)[:, :, None, :, None]
    return (shaped * factor).reshape(aux_rows, occ_cols, vir_cols)


def spread_sum(row_term, total_rows):
    wide_count = lax.axis_size("wide")
    narrow_count = lax.axis_size("narrow")
    own_rows = total_rows // (wide_count * narrow_count)
    full_term = row_term(0, total_rows)
    columns = full_term.shape[1]
    shaped = full_term.reshape(wide_count, narrow_count * own_rows, columns)
    parts = lax.all_to_all(shaped, "wide", split_axis=0, concat_axis=0, tiled=True)
    result = jnp.sum(parts, axis=0)
    if narrow_count > 1:
        result = lax.psum_scatter(result, "narrow", scatter_dimension=0, tiled=True)
    return result


def local(gamma_tensor, three_center, gamma_blocks, center_blocks):
    wide_count = lax.axis_size("wide")
    narrow_count = lax.axis_size("narrow")
    gamma_local = apply_blocks(gamma_tensor, gamma_blocks)
    center_local = apply_blocks(three_center, center_blocks)
    total_aux = gamma_tensor.shape[0] * wide_count
    total_occ = gamma_tensor.shape[1]
    total_vir = gamma_tensor.shape[2] * narrow_count
    occ_scale = -1.0 / math.sqrt(total_aux * total_vir)
    aux_scale = 1.0 / math.sqrt(total_occ * total_vir)

    def occ_term(first_row, row_count):
        product = lax.dot_general(
            gamma_local,
            center_local,
            (((0, 2), (0, 2)), ((), ())),
            preferred_element_type=jnp.float32,
        )
        return product * occ_scale

    density_occ = spread_sum(occ_term, total_occ)
    moved_pair = (
        lax.all_to_all(gamma_local, "wide", split_axis=1, concat_axis=0, tiled=True),
        lax.all_to_all(center_local, "wide", split_axis=1, concat_axis=0, tiled=True),
    )
    gamma_occ, center_occ = moved_pair

    def aux_term(first_row, row_count):
        product = lax.dot_general(
            gamma_occ, center_occ, (((1, 2), (1, 2)), ((), ())), preferred_element_type=jnp.float32
        )
        return product * aux_scale

    gamma_aux = spread_sum(aux_term, total_aux)
    return (density_occ, gamma_aux)


def solution(mesh):
    in_specs = (
        P(("groups", "wide"), None, "narrow"),
        P(("groups", "wide"), None, "narrow"),
        P(("groups", "wide"), None, "narrow"),
        P(("groups", "wide"), None, "narrow"),
    )
    out_specs = (P(("groups", "wide", "narrow"), None), P(("groups", "wide", "narrow"), None))
    return jax.shard_map(local, mesh=mesh, in_specs=in_specs, out_specs=out_specs, check_vma=False)
```

```python
import functools
import math

import jax
import jax.numpy as jnp
from jax import lax
from jax.experimental import pallas as pl
from jax.experimental.pallas import tpu as pltpu
from jax.sharding import PartitionSpec as P

BLK = 64
ROWS = 16
LANES = 128
MESH = pl.DeviceIdType.MESH
F32 = jnp.float32
BF16 = jnp.bfloat16
NT = (((1,), (1,)), ((), ()))


def kernel(
    n, occ_scale, aux_scale,
    g_ref, c_ref, gb_ref, cb_ref, occ_ref, aux_ref,
    mask, keep, stage, send, recv, gram, occ_part, occ_recv, aux_part, aux_recv,
    send_sem, recv_sem, occ_send_sem, occ_recv_sem, aux_send_sem, aux_recv_sem,
):
    me = lax.axis_index("wide")
    aux, occ, vir = g_ref.shape
    blocks = occ // BLK
    row_parts = occ // ROWS
    lane_parts = n // row_parts
    width = vir // lane_parts
    own_occ = occ // n

    def partner(step):
        half = (step + 1) // 2
        sign = 1 - 2 * (step % 2)
        return lax.rem(me + n // 2 + sign * half + n, n)

    barrier = pltpu.get_barrier_semaphore()

    @pl.loop(0, n - 1)
    def _(step):
        pl.semaphore_signal(barrier, inc=1, device_id={"wide": partner(step)}, device_id_type=MESH)

    spread = (
        lax.broadcasted_iota(jnp.int32, (vir // BLK, vir), 1) // BLK
        == lax.broadcasted_iota(jnp.int32, (vir // BLK, vir), 0)
    ).astype(F32)
    for t, b_ref in enumerate((gb_ref, cb_ref)):
        for p in range(aux):
            lines = jnp.dot(b_ref[p].astype(F32), spread, preferred_element_type=F32)
            for b in range(blocks):
                mask[t, p, b] = jnp.broadcast_to(lines[b : b + 1], (8, vir))

    def prepare(dest, out):
        row = pl.multiple_of((dest // lane_parts) * ROWS, ROWS)
        block = (dest // lane_parts) * ROWS // BLK
        for w in range(width // LANES):
            lane = pl.multiple_of((dest % lane_parts) * width + w * LANES, LANES)
            for t, src in enumerate((g_ref, c_ref)):
                for p in range(aux):
                    x = src[p, pl.ds(row, ROWS), pl.ds(lane, LANES)].astype(F32)
                    m = mask[t, p, block, :, pl.ds(lane, LANES)]
                    y = x * jnp.concatenate([m] * (ROWS // 8), axis=0)
                    keep[t, p, pl.ds(row, ROWS), pl.ds(lane, LANES)] = y.astype(BF16)
                    stage[w, pl.ds(t * aux + p, ROWS, stride=2 * aux), :] = y
            for i in range(ROWS):
                piece = stage[w, i * 2 * aux : (i + 1) * 2 * aux, :]
                at = i * width + w * LANES
                out[:, at : at + LANES] = piece.astype(BF16)

    def moved(peer, slot):
        return pltpu.make_async_remote_copy(
            src_ref=send.at[peer], dst_ref=recv.at[slot], send_sem=send_sem.at[peer],
            recv_sem=recv_sem.at[slot], device_id={"wide": peer}, device_id_type=MESH)

    def occ_moved(peer, slot):
        return pltpu.make_async_remote_copy(
            src_ref=occ_part.at[peer], dst_ref=occ_recv.at[slot], send_sem=occ_send_sem.at[peer],
            recv_sem=occ_recv_sem.at[slot], device_id={"wide": peer}, device_id_type=MESH)

    def aux_moved(peer, slot):
        return pltpu.make_async_remote_copy(
            src_ref=aux_part.at[peer], dst_ref=aux_recv.at[slot], send_sem=aux_send_sem.at[peer],
            recv_sem=aux_recv_sem.at[slot], device_id={"wide": peer}, device_id_type=MESH)

    pl.semaphore_wait(barrier, n - 1)

    @pl.loop(0, n - 1)
    def _(step):
        dest = partner(step)
        prepare(dest, send.at[dest])
        moved(dest, me).start()

    prepare(me, recv.at[me])

    def occ_step(p, total):
        return total + lax.dot_general(keep[0, p], keep[1, p], NT, preferred_element_type=F32)

    total = lax.fori_loop(0, aux, occ_step, jnp.zeros((occ, occ), F32)) * occ_scale
    for d in range(n):
        occ_part[d] = total[d * own_occ : (d + 1) * own_occ]
    occ_recv[me] = occ_part[me]

    @pl.loop(0, n - 1)
    def _(step):
        occ_moved(partner(step), me).start()

    @pl.loop(0, n - 1)
    def _(step):
        peer = partner(step)
        moved(peer, peer).wait_recv()

    depth = ROWS * width
    cut = depth // 4
    rows = n * 2 * aux
    gram[...] = jnp.zeros_like(gram)

    @pl.loop(0, depth // cut)
    def _(k):
        x = recv[:, :, pl.ds(pl.multiple_of(k * cut, LANES), cut)].reshape(rows, cut)
        gram[...] += lax.dot_general(x, x, NT, preferred_element_type=F32)

    product = gram[...].reshape(n, 2 * aux, rows)[:, :aux].reshape(n * aux, rows)
    r = lax.broadcasted_iota(jnp.int32, (rows, n * aux), 0)
    q = lax.broadcasted_iota(jnp.int32, (rows, n * aux), 1)
    pick = (r == (q // aux) * (2 * aux) + aux + q % aux).astype(F32)
    picked = jnp.dot(product, pick, precision=lax.Precision.HIGHEST, preferred_element_type=F32)
    aux_part[...] = (picked * aux_scale).reshape(n, aux, n * aux)
    aux_recv[me] = aux_part[me]

    @pl.loop(0, n - 1)
    def _(step):
        aux_moved(partner(step), me).start()

    @pl.loop(0, n - 1)
    def _(step):
        peer = partner(step)
        occ_moved(peer, peer).wait_recv()

    occ_ref[...] = jnp.sum(occ_recv[...], axis=0)

    @pl.loop(0, n - 1)
    def _(step):
        peer = partner(step)
        moved(peer, peer).wait_send()
        occ_moved(peer, peer).wait_send()

    @pl.loop(0, n - 1)
    def _(step):
        peer = partner(step)
        aux_moved(peer, peer).wait_recv()

    aux_ref[...] = jnp.sum(aux_recv[...], axis=0)

    @pl.loop(0, n - 1)
    def _(step):
        peer = partner(step)
        aux_moved(peer, peer).wait_send()


def local(gamma_tensor, three_center, gamma_blocks, center_blocks):
    n = lax.axis_size("wide")
    narrow = lax.axis_size("narrow")
    aux, occ, vir = gamma_tensor.shape
    occ_scale = -1.0 / math.sqrt(aux * n * vir * narrow)
    aux_scale = 1.0 / math.sqrt(occ * vir * narrow)
    width = vir // (n // (occ // ROWS))
    rows = n * 2 * aux
    dma = pltpu.SemaphoreType.DMA((n,))
    density_occ, gamma_aux = pl.pallas_call(
        functools.partial(kernel, n, occ_scale, aux_scale),
        out_shape=(
            jax.ShapeDtypeStruct((occ // n, occ), F32),
            jax.ShapeDtypeStruct((aux, n * aux), F32),
        ),
        in_specs=[pl.BlockSpec(memory_space=pltpu.VMEM)] * 4,
        out_specs=(pl.BlockSpec(memory_space=pltpu.VMEM),) * 2,
        scratch_shapes=[
            pltpu.VMEM((2, aux, occ // BLK, 8, vir), F32),
            pltpu.VMEM((2, aux, occ, vir), BF16),
            pltpu.VMEM((width // LANES, ROWS * 2 * aux, LANES), F32),
            pltpu.VMEM((n, 2 * aux, ROWS * width), BF16),
            pltpu.VMEM((n, 2 * aux, ROWS * width), BF16),
            pltpu.VMEM((rows, rows), F32),
            pltpu.VMEM((n, occ // n, occ), F32),
            pltpu.VMEM((n, occ // n, occ), F32),
            pltpu.VMEM((n, aux, n * aux), F32),
            pltpu.VMEM((n, aux, n * aux), F32),
            dma, dma, dma, dma, dma, dma,
        ],
        compiler_params=pltpu.CompilerParams(
            collective_id=0, has_side_effects=True, vmem_limit_bytes=56 * 1024 * 1024
        ),
    )(gamma_tensor, three_center, gamma_blocks, center_blocks)
    if narrow > 1:
        density_occ = lax.psum_scatter(density_occ, "narrow", scatter_dimension=0, tiled=True)
        gamma_aux = lax.psum_scatter(gamma_aux, "narrow", scatter_dimension=0, tiled=True)
    return (density_occ, gamma_aux)


def solution(mesh):
    spread = P(("groups", "wide"), None, "narrow")
    out = P(("groups", "wide", "narrow"), None)
    return jax.shard_map(
        local, mesh=mesh, in_specs=(spread,) * 4, out_specs=(out, out), check_vma=False
    )
```

```python
import functools
import math

import jax
import jax.numpy as jnp
from jax import lax
from jax.experimental import pallas as pl
from jax.experimental.pallas import tpu as pltpu
from jax.sharding import PartitionSpec as P

BLK = 64
ROWS = 16
LANES = 128
MESH = pl.DeviceIdType.MESH
F32 = jnp.float32
BF16 = jnp.bfloat16
NT = (((1,), (1,)), ((), ()))


def kernel(
    n, occ_scale, aux_scale,
    g_hbm, c_hbm, gb_ref, cb_ref, occ_ref, aux_ref,
    g_ref, c_ref, mask, keep, stage, send, recv, g_all, c_all,
    occ_part, occ_recv, occ_mid, occ_far, aux_part, aux_recv, aux_mid, aux_far,
    load_sem, send_sem, recv_sem, occ_send_sem, occ_recv_sem, aux_send_sem, aux_recv_sem, far_sem,
):
    me = lax.axis_index("wide")
    aux, occ, vir = g_ref.shape
    blocks = occ // BLK
    row_parts = occ // ROWS
    lane_parts = n // row_parts
    width = vir // lane_parts
    own_occ = occ // n
    half = n // 2
    side = lax.div(me, half)
    place = lax.rem(me, half)
    mirror = (1 - side) * half + place

    def flip(index, step, bits):
        peer = 0
        for b in range(bits):
            both = lax.div(index, 1 << b) + lax.div(step, 1 << (bits - 1 - b))
            peer += lax.rem(both, 2) * (1 << b)
        return peer

    def partner(step):
        return flip(me, step, n.bit_length() - 1)

    def neighbour(step):
        return flip(place, step, half.bit_length() - 1)

    loads = [
        pltpu.make_async_copy(g_hbm, g_ref, load_sem.at[0]),
        pltpu.make_async_copy(c_hbm, c_ref, load_sem.at[1]),
    ]
    for load in loads:
        load.start()

    barrier = pltpu.get_barrier_semaphore()

    @pl.loop(1, n)
    def _(step):
        pl.semaphore_signal(barrier, inc=1, device_id={"wide": partner(step)}, device_id_type=MESH)

    spread = (
        lax.broadcasted_iota(jnp.int32, (vir // BLK, vir), 1) // BLK
        == lax.broadcasted_iota(jnp.int32, (vir // BLK, vir), 0)
    ).astype(F32)
    for t, b_ref in enumerate((gb_ref, cb_ref)):
        for p in range(aux):
            lines = jnp.dot(b_ref[p].astype(F32), spread, preferred_element_type=F32)
            for b in range(blocks):
                mask[t, p, b] = jnp.broadcast_to(lines[b : b + 1], (8, vir))

    def prepare(dest, out):
        row = pl.multiple_of((dest // lane_parts) * ROWS, ROWS)
        block = (dest // lane_parts) * ROWS // BLK
        for w in range(width // LANES):
            lane = pl.multiple_of((dest % lane_parts) * width + w * LANES, LANES)
            for t, src in enumerate((g_ref, c_ref)):
                for p in range(aux):
                    x = src[p, pl.ds(row, ROWS), pl.ds(lane, LANES)].astype(F32)
                    m = mask[t, p, block, :, pl.ds(lane, LANES)]
                    y = x * jnp.concatenate([m] * (ROWS // 8), axis=0)
                    keep[t, p, pl.ds(row, ROWS), pl.ds(lane, LANES)] = y.astype(BF16)
                    stage[w, pl.ds(t * aux + p, ROWS, stride=2 * aux), :] = y
            for i in range(ROWS):
                piece = stage[w, i * 2 * aux : (i + 1) * 2 * aux, :]
                at = i * width + w * LANES
                out[:, at : at + LANES] = piece.astype(BF16)

    def moved(peer, slot):
        return pltpu.make_async_remote_copy(
            src_ref=send.at[peer], dst_ref=recv.at[slot], send_sem=send_sem.at[peer],
            recv_sem=recv_sem.at[slot], device_id={"wide": peer}, device_id_type=MESH)

    def summed(part, received, sems):
        def one(peer, slot):
            return pltpu.make_async_remote_copy(
                src_ref=part.at[peer], dst_ref=received.at[slot], send_sem=sems[0].at[peer],
                recv_sem=sems[1].at[slot], device_id={"wide": side * half + peer},
                device_id_type=MESH)
        return one

    def across(mid, far, slot):
        return pltpu.make_async_remote_copy(
            src_ref=mid.at[1 - side], dst_ref=far, send_sem=far_sem.at[slot],
            recv_sem=far_sem.at[slot + 1], device_id={"wide": mirror}, device_id_type=MESH)

    occ_moved = summed(occ_part, occ_recv, (occ_send_sem, occ_recv_sem))
    aux_moved = summed(aux_part, aux_recv, (aux_send_sem, aux_recv_sem))
    occ_across = across(occ_mid, occ_far, 0)
    aux_across = across(aux_mid, aux_far, 2)

    for load in loads:
        load.wait()
    first = partner(1)
    prepare(first, send.at[first])
    pl.semaphore_wait(barrier, n - 1)
    moved(first, me).start()

    @pl.loop(2, n)
    def _(step):
        dest = partner(step)
        prepare(dest, send.at[dest])
        moved(dest, me).start()

    prepare(me, recv.at[me])

    def occ_step(p, total):
        return total + lax.dot_general(keep[0, p], keep[1, p], NT, preferred_element_type=F32)

    total = lax.fori_loop(0, aux, occ_step, jnp.zeros((occ, occ), F32)) * occ_scale
    for d in range(n):
        occ_part[d % half, d // half] = total[d * own_occ : (d + 1) * own_occ]
    occ_recv[place] = occ_part[place]

    @pl.loop(1, half)
    def _(step):
        occ_moved(neighbour(step), place).start()

    @pl.loop(1, half)
    def _(step):
        peer = partner(step)
        moved(peer, peer).wait_recv()

    depth = ROWS * width

    @pl.loop(half, n)
    def _(step):
        peer = partner(step)
        moved(peer, peer).wait_recv()
        pair = lax.div(peer, 2)
        for k in range(0, depth, 512):
            x = recv[2 * pair, :, k : k + 512].astype(F32)
            y = recv[2 * pair + 1, :, k : k + 512].astype(F32)
            g_all[pair, :, k : k + 512] = jnp.concatenate([x[:aux], y[:aux]], axis=0).astype(BF16)
            c_all[pair, :, k : k + 512] = jnp.concatenate([x[aux:], y[aux:]], axis=0).astype(BF16)

    product = lax.dot_general(
        g_all[...].reshape(n * aux, depth), c_all[...].reshape(n * aux, depth), NT,
        preferred_element_type=F32,
    )
    spread_rows = (product * aux_scale).reshape(2, half, aux, n * aux)
    for h in range(2):
        aux_part[:, h] = spread_rows[h]

    @pl.loop(1, half)
    def _(step):
        aux_moved(neighbour(step), place).start()

    aux_recv[place] = aux_part[place]

    @pl.loop(1, half)
    def _(step):
        peer = neighbour(step)
        occ_moved(peer, peer).wait_recv()

    occ_mid[...] = jnp.sum(occ_recv[...], axis=0)
    occ_across.start()

    @pl.loop(1, n)
    def _(step):
        peer = partner(step)
        moved(peer, peer).wait_send()

    @pl.loop(1, half)
    def _(step):
        peer = neighbour(step)
        occ_moved(peer, peer).wait_send()

    @pl.loop(1, half)
    def _(step):
        peer = neighbour(step)
        aux_moved(peer, peer).wait_recv()

    aux_mid[...] = jnp.sum(aux_recv[...], axis=0)
    aux_across.start()

    @pl.loop(1, half)
    def _(step):
        peer = neighbour(step)
        aux_moved(peer, peer).wait_send()

    occ_across.wait()
    occ_ref[...] = occ_mid[side] + occ_far[...]
    aux_across.wait()
    aux_ref[...] = aux_mid[side] + aux_far[...]


def local(gamma_tensor, three_center, gamma_blocks, center_blocks):
    n = lax.axis_size("wide")
    narrow = lax.axis_size("narrow")
    aux, occ, vir = gamma_tensor.shape
    occ_scale = -1.0 / math.sqrt(aux * n * vir * narrow)
    aux_scale = 1.0 / math.sqrt(occ * vir * narrow)
    width = vir // (n // (occ // ROWS))
    half = n // 2
    own_occ = occ // n
    part_dma = pltpu.SemaphoreType.DMA((half,))
    dma = pltpu.SemaphoreType.DMA((n,))
    density_occ, gamma_aux = pl.pallas_call(
        functools.partial(kernel, n, occ_scale, aux_scale),
        out_shape=(
            jax.ShapeDtypeStruct((occ // n, occ), F32),
            jax.ShapeDtypeStruct((aux, n * aux), F32),
        ),
        in_specs=[pl.BlockSpec(memory_space=pl.ANY)] * 2
        + [pl.BlockSpec(memory_space=pltpu.VMEM)] * 2,
        out_specs=(pl.BlockSpec(memory_space=pltpu.VMEM),) * 2,
        scratch_shapes=[
            pltpu.VMEM((aux, occ, vir), BF16),
            pltpu.VMEM((aux, occ, vir), BF16),
            pltpu.VMEM((2, aux, occ // BLK, 8, vir), F32),
            pltpu.VMEM((2, aux, occ, vir), BF16),
            pltpu.VMEM((width // LANES, ROWS * 2 * aux, LANES), F32),
            pltpu.VMEM((n, 2 * aux, ROWS * width), BF16),
            pltpu.VMEM((n, 2 * aux, ROWS * width), BF16),
            pltpu.VMEM((half, 2 * aux, ROWS * width), BF16),
            pltpu.VMEM((half, 2 * aux, ROWS * width), BF16),
            pltpu.VMEM((half, 2, own_occ, occ), F32),
            pltpu.VMEM((half, 2, own_occ, occ), F32),
            pltpu.VMEM((2, own_occ, occ), F32),
            pltpu.VMEM((own_occ, occ), F32),
            pltpu.VMEM((half, 2, aux, n * aux), F32),
            pltpu.VMEM((half, 2, aux, n * aux), F32),
            pltpu.VMEM((2, aux, n * aux), F32),
            pltpu.VMEM((aux, n * aux), F32),
            pltpu.SemaphoreType.DMA((2,)),
            dma, dma, part_dma, part_dma, part_dma, part_dma,
            pltpu.SemaphoreType.DMA((4,)),
        ],
        compiler_params=pltpu.CompilerParams(
            collective_id=0, has_side_effects=True, vmem_limit_bytes=56 * 1024 * 1024
        ),
    )(gamma_tensor, three_center, gamma_blocks, center_blocks)
    if narrow > 1:
        density_occ = lax.psum_scatter(density_occ, "narrow", scatter_dimension=0, tiled=True)
        gamma_aux = lax.psum_scatter(gamma_aux, "narrow", scatter_dimension=0, tiled=True)
    return (density_occ, gamma_aux)


def solution(mesh):
    spread = P(("groups", "wide"), None, "narrow")
    out = P(("groups", "wide", "narrow"), None)
    return jax.shard_map(
        local, mesh=mesh, in_specs=(spread,) * 4, out_specs=(out, out), check_vma=False
    )
```

```python
import functools
import math

import jax
import jax.numpy as jnp
from jax import lax
from jax.experimental import pallas as pl
from jax.experimental.pallas import tpu as pltpu
from jax.sharding import PartitionSpec as P

BLK = 64
ROWS = 16
LANES = 128
MESH = pl.DeviceIdType.MESH
F32 = jnp.float32
BF16 = jnp.bfloat16
NT = (((1,), (1,)), ((), ()))


def kernel(
    n, occ_scale, aux_scale,
    g_hbm, c_hbm, gb_ref, cb_ref, occ_ref, aux_ref,
    g_ref, c_ref, mask, keep, stage, send, recv, g_all, c_all,
    occ_part, occ_recv, occ_mid, occ_far, aux_part, aux_recv, aux_mid, aux_far,
    load_sem, send_sem, recv_sem, occ_sem, aux_sem, far_sem,
):
    me = lax.axis_index("wide")
    aux, occ, vir = g_ref.shape
    blocks = occ // BLK
    row_parts = occ // ROWS
    lane_parts = n // row_parts
    width = vir // lane_parts
    own_occ = occ // n
    half = n // 2
    side = lax.div(me, half)
    place = lax.rem(me, half)
    mirror = (1 - side) * half + place

    def flip(index, step, bits):
        peer = 0
        for b in range(bits):
            both = lax.div(index, 1 << b) + lax.div(step, 1 << (bits - 1 - b))
            peer += lax.rem(both, 2) * (1 << b)
        return peer

    def partner(step):
        return flip(me, step, n.bit_length() - 1)

    def neighbour(step):
        return flip(place, step, half.bit_length() - 1)

    loads = [
        pltpu.make_async_copy(g_hbm, g_ref, load_sem.at[0]),
        pltpu.make_async_copy(c_hbm, c_ref, load_sem.at[1]),
    ]
    for load in loads:
        load.start()

    barrier = pltpu.get_barrier_semaphore()

    @pl.loop(1, n)
    def _(step):
        pl.semaphore_signal(barrier, inc=1, device_id={"wide": partner(step)}, device_id_type=MESH)

    spread = (
        lax.broadcasted_iota(jnp.int32, (vir // BLK, vir), 1) // BLK
        == lax.broadcasted_iota(jnp.int32, (vir // BLK, vir), 0)
    ).astype(F32)
    for t, b_ref in enumerate((gb_ref, cb_ref)):
        for p in range(aux):
            lines = jnp.dot(b_ref[p].astype(F32), spread, preferred_element_type=F32)
            for b in range(blocks):
                mask[t, p, b] = jnp.broadcast_to(lines[b : b + 1], (8, vir))

    def prepare(dest, out):
        row = pl.multiple_of((dest // lane_parts) * ROWS, ROWS)
        block = (dest // lane_parts) * ROWS // BLK
        for w in range(width // LANES):
            lane = pl.multiple_of((dest % lane_parts) * width + w * LANES, LANES)
            for t, src in enumerate((g_ref, c_ref)):
                for p in range(aux):
                    x = src[p, pl.ds(row, ROWS), pl.ds(lane, LANES)].astype(F32)
                    m = mask[t, p, block, :, pl.ds(lane, LANES)]
                    y = x * jnp.concatenate([m] * (ROWS // 8), axis=0)
                    keep[t, p, pl.ds(row, ROWS), pl.ds(lane, LANES)] = y.astype(BF16)
                    stage[w, pl.ds(t * aux + p, ROWS, stride=2 * aux), :] = y
            for i in range(ROWS):
                piece = stage[w, i * 2 * aux : (i + 1) * 2 * aux, :]
                at = i * width + w * LANES
                out[:, at : at + LANES] = piece.astype(BF16)

    def moved(peer, step):
        return pltpu.make_async_remote_copy(
            src_ref=send.at[step], dst_ref=recv.at[step], send_sem=send_sem.at[0],
            recv_sem=recv_sem.at[step], device_id={"wide": peer}, device_id_type=MESH)

    def take(buffer, sem):
        pltpu.make_async_copy(buffer, buffer, sem).wait()

    def exchange(part, received, sems):
        @pl.loop(1, half)
        def _(step):
            peer = neighbour(step)
            pltpu.make_async_remote_copy(
                src_ref=part.at[peer], dst_ref=received.at[step], send_sem=sems.at[0],
                recv_sem=sems.at[1], device_id={"wide": side * half + peer},
                device_id_type=MESH).start()

        received[0] = part[place]

    def across(mid, far, slot):
        return pltpu.make_async_remote_copy(
            src_ref=mid.at[1 - side], dst_ref=far, send_sem=far_sem.at[slot],
            recv_sem=far_sem.at[slot + 1], device_id={"wide": mirror}, device_id_type=MESH)

    occ_across = across(occ_mid, occ_far, 0)
    aux_across = across(aux_mid, aux_far, 2)

    for load in loads:
        load.wait()
    first = partner(1)
    prepare(first, send.at[1])
    pl.semaphore_wait(barrier, n - 1)
    moved(first, 1).start()

    @pl.loop(2, n)
    def _(step):
        dest = partner(step)
        prepare(dest, send.at[step])
        moved(dest, step).start()

    prepare(me, recv.at[0])

    def occ_step(p, total):
        return total + lax.dot_general(keep[0, p], keep[1, p], NT, preferred_element_type=F32)

    total = lax.fori_loop(0, aux, occ_step, jnp.zeros((occ, occ), F32)) * occ_scale
    for d in range(n):
        occ_part[d % half, d // half] = total[d * own_occ : (d + 1) * own_occ]
    exchange(occ_part, occ_recv, occ_sem)

    @pl.loop(1, half)
    def _(step):
        take(recv.at[step], recv_sem.at[step])

    depth = ROWS * width
    odd = lax.rem(me, 2)

    @pl.loop(half, n)
    def _(step):
        take(recv.at[step], recv_sem.at[step])
        pair = lax.div(partner(step), 2)
        even_slot = step - half + half * odd
        odd_slot = step - half * odd
        for k in range(0, depth, 512):
            x = recv[even_slot, :, k : k + 512].astype(F32)
            y = recv[odd_slot, :, k : k + 512].astype(F32)
            g_all[pair, :, k : k + 512] = jnp.concatenate([x[:aux], y[:aux]], axis=0).astype(BF16)
            c_all[pair, :, k : k + 512] = jnp.concatenate([x[aux:], y[aux:]], axis=0).astype(BF16)

    product = lax.dot_general(
        g_all[...].reshape(n * aux, depth), c_all[...].reshape(n * aux, depth), NT,
        preferred_element_type=F32,
    )
    spread_rows = (product * aux_scale).reshape(2, half, aux, n * aux)
    for h in range(2):
        aux_part[:, h] = spread_rows[h]

    exchange(aux_part, aux_recv, aux_sem)
    others = pl.ds(1, half - 1)
    take(occ_recv.at[others], occ_sem.at[1])
    occ_mid[...] = jnp.sum(occ_recv[...], axis=0)
    occ_across.start()
    take(send.at[pl.ds(1, n - 1)], send_sem.at[0])
    take(occ_recv.at[others], occ_sem.at[0])
    take(aux_recv.at[others], aux_sem.at[1])
    aux_mid[...] = jnp.sum(aux_recv[...], axis=0)
    aux_across.start()
    take(aux_recv.at[others], aux_sem.at[0])
    occ_across.wait()
    occ_ref[...] = occ_mid[side] + occ_far[...]
    aux_across.wait()
    aux_ref[...] = aux_mid[side] + aux_far[...]


def hand_over(occ_in, aux_in, occ_out, aux_out):
    occ_out[...] = occ_in[...]
    aux_out[...] = aux_in[...]


def local(gamma_tensor, three_center, gamma_blocks, center_blocks):
    n = lax.axis_size("wide")
    narrow = lax.axis_size("narrow")
    aux, occ, vir = gamma_tensor.shape
    occ_scale = -1.0 / math.sqrt(aux * n * vir * narrow)
    aux_scale = 1.0 / math.sqrt(occ * vir * narrow)
    width = vir // (n // (occ // ROWS))
    half = n // 2
    own_occ = occ // n
    density_occ, gamma_aux = pl.pallas_call(
        functools.partial(kernel, n, occ_scale, aux_scale),
        out_shape=(
            jax.ShapeDtypeStruct((occ // n, occ), F32),
            jax.ShapeDtypeStruct((aux, n * aux), F32),
        ),
        in_specs=[pl.BlockSpec(memory_space=pl.ANY)] * 2
        + [pl.BlockSpec(memory_space=pltpu.VMEM)] * 2,
        out_specs=(pl.BlockSpec(memory_space=pltpu.VMEM),) * 2,
        scratch_shapes=[
            pltpu.VMEM((aux, occ, vir), BF16),
            pltpu.VMEM((aux, occ, vir), BF16),
            pltpu.VMEM((2, aux, occ // BLK, 8, vir), F32),
            pltpu.VMEM((2, aux, occ, vir), BF16),
            pltpu.VMEM((width // LANES, ROWS * 2 * aux, LANES), F32),
            pltpu.VMEM((n, 2 * aux, ROWS * width), BF16),
            pltpu.VMEM((n, 2 * aux, ROWS * width), BF16),
            pltpu.VMEM((half, 2 * aux, ROWS * width), BF16),
            pltpu.VMEM((half, 2 * aux, ROWS * width), BF16),
            pltpu.VMEM((half, 2, own_occ, occ), F32),
            pltpu.VMEM((half, 2, own_occ, occ), F32),
            pltpu.VMEM((2, own_occ, occ), F32),
            pltpu.VMEM((own_occ, occ), F32),
            pltpu.VMEM((half, 2, aux, n * aux), F32),
            pltpu.VMEM((half, 2, aux, n * aux), F32),
            pltpu.VMEM((2, aux, n * aux), F32),
            pltpu.VMEM((aux, n * aux), F32),
            pltpu.SemaphoreType.DMA((2,)),
            pltpu.SemaphoreType.DMA((1,)),
            pltpu.SemaphoreType.DMA((n,)),
            pltpu.SemaphoreType.DMA((2,)),
            pltpu.SemaphoreType.DMA((2,)),
            pltpu.SemaphoreType.DMA((4,)),
        ],
        compiler_params=pltpu.CompilerParams(
            collective_id=0, has_side_effects=True, vmem_limit_bytes=56 * 1024 * 1024
        ),
    )(gamma_tensor, three_center, gamma_blocks, center_blocks)
    if narrow > 1:
        density_occ = lax.psum_scatter(density_occ, "narrow", scatter_dimension=0, tiled=True)
        gamma_aux = lax.psum_scatter(gamma_aux, "narrow", scatter_dimension=0, tiled=True)
    else:
        density_occ, gamma_aux = pl.pallas_call(
            hand_over,
            out_shape=(
                jax.ShapeDtypeStruct(density_occ.shape, F32),
                jax.ShapeDtypeStruct(gamma_aux.shape, F32),
            ),
            in_specs=[pl.BlockSpec(memory_space=pltpu.VMEM)] * 2,
            out_specs=(pl.BlockSpec(memory_space=pltpu.VMEM),) * 2,
        )(density_occ, gamma_aux)
    return (density_occ, gamma_aux)


def solution(mesh):
    spread = P(("groups", "wide"), None, "narrow")
    out = P(("groups", "wide", "narrow"), None)
    return jax.shard_map(
        local, mesh=mesh, in_specs=(spread,) * 4, out_specs=(out, out), check_vma=False
    )
```

```python
import functools
import math

import jax
import jax.numpy as jnp
from jax import lax
from jax.experimental import pallas as pl
from jax.experimental.pallas import tpu as pltpu
from jax.sharding import PartitionSpec as P

BLK = 64
ROWS = 16
LANES = 128
SIDES = 16
MESH = pl.DeviceIdType.MESH
F32 = jnp.float32
BF16 = jnp.bfloat16
NT = (((1,), (1,)), ((), ()))


def kernel(
    n, sides, occ_scale, aux_scale,
    g_hbm, c_hbm, gb_ref, cb_ref, occ_ref, aux_ref,
    g_ref, c_ref, mask, keep, stage, send, recv, g_all, c_all,
    occ_part, occ_recv, occ_mid, occ_far, aux_part, aux_recv, aux_mid, aux_far,
    load_sem, send_sem, recv_sem, occ_sem, aux_sem, occ_far_sem, aux_far_sem,
):
    me = lax.axis_index("wide")
    aux, occ, vir = g_ref.shape
    blocks = occ // BLK
    row_parts = occ // ROWS
    lane_parts = n // row_parts
    width = vir // lane_parts
    own_occ = occ // n
    half = n // 2
    group = n // sides
    side = lax.div(me, group)
    place = lax.rem(me, group)

    def flip(index, step, bits):
        peer = 0
        for b in range(bits):
            both = lax.div(index, 1 << b) + lax.div(step, 1 << (bits - 1 - b))
            peer += lax.rem(both, 2) * (1 << b)
        return peer

    def partner(step):
        return flip(me, step, n.bit_length() - 1)

    def neighbour(step):
        return flip(place, step, group.bit_length() - 1)

    loads = [
        pltpu.make_async_copy(g_hbm, g_ref, load_sem.at[0]),
        pltpu.make_async_copy(c_hbm, c_ref, load_sem.at[1]),
    ]

    barrier = pltpu.get_barrier_semaphore()

    @pl.loop(1, n)
    def _(step):
        peer = lax.rem(me + step, n)
        pl.semaphore_signal(barrier, inc=1, device_id={"wide": peer}, device_id_type=MESH)

    for load in loads:
        load.start()
    spread = (
        lax.broadcasted_iota(jnp.int32, (vir // BLK, vir), 1) // BLK
        == lax.broadcasted_iota(jnp.int32, (vir // BLK, vir), 0)
    ).astype(F32)
    for t, b_ref in enumerate((gb_ref, cb_ref)):
        for p in range(aux):
            lines = jnp.dot(b_ref[p].astype(F32), spread, preferred_element_type=F32)
            for b in range(blocks):
                mask[t, p, b] = jnp.broadcast_to(lines[b : b + 1], (8, vir))

    def prepare(dest, out):
        row = pl.multiple_of((dest // lane_parts) * ROWS, ROWS)
        block = (dest // lane_parts) * ROWS // BLK
        for w in range(width // LANES):
            lane = pl.multiple_of((dest % lane_parts) * width + w * LANES, LANES)
            for t, src in enumerate((g_ref, c_ref)):
                for p in range(aux):
                    x = src[p, pl.ds(row, ROWS), pl.ds(lane, LANES)].astype(F32)
                    m = mask[t, p, block, :, pl.ds(lane, LANES)]
                    y = x * jnp.concatenate([m] * (ROWS // 8), axis=0)
                    keep[t, p, pl.ds(row, ROWS), pl.ds(lane, LANES)] = y.astype(BF16)
                    stage[w, pl.ds(t * aux + p, ROWS, stride=2 * aux), :] = y
            for i in range(ROWS):
                piece = stage[w, i * 2 * aux : (i + 1) * 2 * aux, :]
                at = i * width + w * LANES
                out[:, at : at + LANES] = piece.astype(BF16)

    def moved(peer, step):
        return pltpu.make_async_remote_copy(
            src_ref=send.at[step], dst_ref=recv.at[step], send_sem=send_sem.at[0],
            recv_sem=recv_sem.at[step], device_id={"wide": peer}, device_id_type=MESH)

    def take(buffer, sem):
        pltpu.make_async_copy(buffer, buffer, sem).wait()

    def exchange(part, received, sems):
        @pl.loop(1, group)
        def _(step):
            peer = neighbour(step)
            pltpu.make_async_remote_copy(
                src_ref=part.at[peer], dst_ref=received.at[step], send_sem=sems.at[0],
                recv_sem=sems.at[1], device_id={"wide": side * group + peer},
                device_id_type=MESH).start()

        received[0] = part[place]

    def across(mid, far, sems):
        copies = []
        for d in range(1, sides):
            other = lax.rem(side + d, sides)
            copies.append(pltpu.make_async_remote_copy(
                src_ref=mid.at[other], dst_ref=far.at[d - 1], send_sem=sems.at[0, d - 1],
                recv_sem=sems.at[1, d - 1], device_id={"wide": other * group + place},
                device_id_type=MESH))
        return copies

    occ_across = across(occ_mid, occ_far, occ_far_sem)
    aux_across = across(aux_mid, aux_far, aux_far_sem)

    for load in loads:
        load.wait()
    first = partner(1)
    prepare(first, send.at[1])
    pl.semaphore_wait(barrier, n - 1)
    moved(first, 1).start()

    @pl.loop(2, n)
    def _(step):
        dest = partner(step)
        prepare(dest, send.at[step])
        moved(dest, step).start()

    prepare(me, recv.at[0])

    def occ_step(p, total):
        return total + lax.dot_general(keep[0, p], keep[1, p], NT, preferred_element_type=F32)

    total = lax.fori_loop(0, aux, occ_step, jnp.zeros((occ, occ), F32)) * occ_scale
    for d in range(n):
        occ_part[d % group, d // group] = total[d * own_occ : (d + 1) * own_occ]
    exchange(occ_part, occ_recv, occ_sem)

    @pl.loop(1, half)
    def _(step):
        take(recv.at[step], recv_sem.at[step])

    depth = ROWS * width
    odd = lax.rem(me, 2)

    @pl.loop(half, n)
    def _(step):
        take(recv.at[step], recv_sem.at[step])
        pair = lax.div(partner(step), 2)
        even_slot = step - half + half * odd
        odd_slot = step - half * odd
        for k in range(0, depth, 512):
            x = recv[even_slot, :, k : k + 512].astype(F32)
            y = recv[odd_slot, :, k : k + 512].astype(F32)
            g_all[pair, :, k : k + 512] = jnp.concatenate([x[:aux], y[:aux]], axis=0).astype(BF16)
            c_all[pair, :, k : k + 512] = jnp.concatenate([x[aux:], y[aux:]], axis=0).astype(BF16)

    product = lax.dot_general(
        g_all[...].reshape(n * aux, depth), c_all[...].reshape(n * aux, depth), NT,
        preferred_element_type=F32,
    )
    spread_rows = (product * aux_scale).reshape(sides, group, aux, n * aux)
    for h in range(sides):
        aux_part[:, h] = spread_rows[h]

    exchange(aux_part, aux_recv, aux_sem)
    others = pl.ds(1, group - 1)
    take(occ_recv.at[others], occ_sem.at[1])
    occ_mid[...] = jnp.sum(occ_recv[...], axis=0)
    for copy in occ_across:
        copy.start()
    take(send.at[pl.ds(1, n - 1)], send_sem.at[0])
    take(occ_recv.at[others], occ_sem.at[0])
    take(aux_recv.at[others], aux_sem.at[1])
    aux_mid[...] = jnp.sum(aux_recv[...], axis=0)
    for copy in aux_across:
        copy.start()
    take(aux_recv.at[others], aux_sem.at[0])
    for copy in occ_across:
        copy.wait()
    occ_ref[...] = occ_mid[side] + jnp.sum(occ_far[...], axis=0)
    for copy in aux_across:
        copy.wait()
    aux_ref[...] = aux_mid[side] + jnp.sum(aux_far[...], axis=0)


def hand_over(occ_in, aux_in, occ_out, aux_out):
    occ_out[...] = occ_in[...]
    aux_out[...] = aux_in[...]


def local(gamma_tensor, three_center, gamma_blocks, center_blocks):
    n = lax.axis_size("wide")
    narrow = lax.axis_size("narrow")
    aux, occ, vir = gamma_tensor.shape
    occ_scale = -1.0 / math.sqrt(aux * n * vir * narrow)
    aux_scale = 1.0 / math.sqrt(occ * vir * narrow)
    width = vir // (n // (occ // ROWS))
    half = n // 2
    own_occ = occ // n
    density_occ, gamma_aux = pl.pallas_call(
        functools.partial(kernel, n, SIDES, occ_scale, aux_scale),
        out_shape=(
            jax.ShapeDtypeStruct((occ // n, occ), F32),
            jax.ShapeDtypeStruct((aux, n * aux), F32),
        ),
        in_specs=[pl.BlockSpec(memory_space=pl.ANY)] * 2
        + [pl.BlockSpec(memory_space=pltpu.VMEM)] * 2,
        out_specs=(pl.BlockSpec(memory_space=pltpu.VMEM),) * 2,
        scratch_shapes=[
            pltpu.VMEM((aux, occ, vir), BF16),
            pltpu.VMEM((aux, occ, vir), BF16),
            pltpu.VMEM((2, aux, occ // BLK, 8, vir), F32),
            pltpu.VMEM((2, aux, occ, vir), BF16),
            pltpu.VMEM((width // LANES, ROWS * 2 * aux, LANES), F32),
            pltpu.VMEM((n, 2 * aux, ROWS * width), BF16),
            pltpu.VMEM((n, 2 * aux, ROWS * width), BF16),
            pltpu.VMEM((half, 2 * aux, ROWS * width), BF16),
            pltpu.VMEM((half, 2 * aux, ROWS * width), BF16),
            pltpu.VMEM((n // SIDES, SIDES, own_occ, occ), F32),
            pltpu.VMEM((n // SIDES, SIDES, own_occ, occ), F32),
            pltpu.VMEM((SIDES, own_occ, occ), F32),
            pltpu.VMEM((SIDES - 1, own_occ, occ), F32),
            pltpu.VMEM((n // SIDES, SIDES, aux, n * aux), F32),
            pltpu.VMEM((n // SIDES, SIDES, aux, n * aux), F32),
            pltpu.VMEM((SIDES, aux, n * aux), F32),
            pltpu.VMEM((SIDES - 1, aux, n * aux), F32),
            pltpu.SemaphoreType.DMA((2,)),
            pltpu.SemaphoreType.DMA((1,)),
            pltpu.SemaphoreType.DMA((n,)),
            pltpu.SemaphoreType.DMA((2,)),
            pltpu.SemaphoreType.DMA((2,)),
            pltpu.SemaphoreType.DMA((2, SIDES - 1)),
            pltpu.SemaphoreType.DMA((2, SIDES - 1)),
        ],
        compiler_params=pltpu.CompilerParams(
            collective_id=0, has_side_effects=True, vmem_limit_bytes=56 * 1024 * 1024
        ),
    )(gamma_tensor, three_center, gamma_blocks, center_blocks)
    if narrow > 1:
        density_occ = lax.psum_scatter(density_occ, "narrow", scatter_dimension=0, tiled=True)
        gamma_aux = lax.psum_scatter(gamma_aux, "narrow", scatter_dimension=0, tiled=True)
    else:
        density_occ, gamma_aux = pl.pallas_call(
            hand_over,
            out_shape=(
                jax.ShapeDtypeStruct(density_occ.shape, F32),
                jax.ShapeDtypeStruct(gamma_aux.shape, F32),
            ),
            in_specs=[pl.BlockSpec(memory_space=pltpu.VMEM)] * 2,
            out_specs=(pl.BlockSpec(memory_space=pltpu.VMEM),) * 2,
        )(density_occ, gamma_aux)
    return (density_occ, gamma_aux)


def solution(mesh):
    spread = P(("groups", "wide"), None, "narrow")
    out = P(("groups", "wide", "narrow"), None)
    return jax.shard_map(
        local, mesh=mesh, in_specs=(spread,) * 4, out_specs=(out, out), check_vma=False
    )
```
